512 devices in a mesh: dp: 32 (over y, z_lo), seq: 16 (over x, z_hi, core).
Axes of the slice: x: 4, y: 4, z: 16 (z_hi: 2, z_lo: 8; z = z_hi * 8 + z_lo), core: 2. Of those that a mesh axis runs over, the one named last changes fastest.
Arguments:
- q_in: bfloat16 [65536, 4096], P(('dp', 'seq')), may hold values from -200 to 200
- k_in: bfloat16 [65536, 4096], P(('dp', 'seq')), may hold values from -200 to 200
- v_in: bfloat16 [65536, 4096], P(('dp', 'seq')), may hold values from -6 to 6
- cotangent: bfloat16 [65536, 4096], P(('dp', 'seq')), may hold values from -6 to 6
- owner: int32 [32, 16], P('dp'), may hold values from 0 to 15, each once within a row
- gain_q: float32 [4096], P('seq'), may hold values from 0.1 to 1.9
- gain_k: float32 [4096], P('seq'), may hold values from 0.1 to 1.9
Outputs:
- grad_gain_q: float32 [4096], P(('seq', 'dp'))
- grad_gain_k: float32 [4096], P(('seq', 'dp'))
The draws below stay inside these ranges and needn't reach their ends.
Inputs may be any that keep to these rules, and one draw needn't show every extreme that they name: `owner`: each row is a permutation; slot s belongs to clip s // 8, time span s % 8 of it.
All inputs are finite; a program needn't handle non-finite values.
Results may differ from the reference program's by a relative error of at most 0.03.
Values may be sent and summed in bfloat16 or wider, within the bound.
A program may use at most 64 MiB of HBM per device.

```python
import jax
import jax.numpy as jnp
from jax import lax

HEADS = 32
HEAD_DIM = 128
SPAN_TOK = 128
CLIPS_GRP = 2
HD_ALL = 4096
CLIP_TOK = 1024
GRP_TOK = 2048
TOKENS = 65536
N_DP = 32
N_SEQ = 16


def draw_q_in(key, part):
    key = jax.random.fold_in(key, 3)
    own_key = jax.random.fold_in(key, 0)
    return jax.random.normal(own_key, (TOKENS, HD_ALL), jnp.float32).astype(jnp.bfloat16)


def draw_k_in(key, part):
    key = jax.random.fold_in(key, 5)
    own_key = jax.random.fold_in(key, 0)
    return jax.random.normal(own_key, (TOKENS, HD_ALL), jnp.float32).astype(jnp.bfloat16)


def strengthened(drawn, key, source, target, shards_of, factor):
    owner, partner = [(jnp.arange(drawn.shape[dim]) // (drawn.shape[dim] // shards_of)).reshape([-1 if axis == dim else 1 for axis in range(drawn.ndim)]) for dim in (source, target)]
    chosen = jax.random.permutation(key, shards_of)[partner]
    strong = (owner == chosen) | (owner == (partner + shards_of // 2) % shards_of)
    return jnp.where(strong, factor * drawn, drawn)


def level_of(rng, shape, cuts, least, high):
    def one(position, shards_of):
        heights = jax.random.uniform(jax.random.fold_in(jax.random.fold_in(rng, 6), position), (shards_of,), jnp.float32, least / len(cuts), high / len(cuts))
        return jnp.repeat(jnp.exp(heights), shape[position] // shards_of).reshape((-1,) + (1,) * (len(shape) - position - 1))

    factor_of = one(*cuts[0])
    for cut in cuts[1:]:
        factor_of = factor_of * one(*cut)
    return factor_of


def centred(key, extent, scale, reach, cuts=(), held_as=jnp.bfloat16):
    drawn = scale * jax.random.normal(key, extent, jnp.float32)
    if cuts:
        drawn = drawn * level_of(key, extent, cuts, -0.22, 0.18)
    return jnp.clip(drawn, -reach, reach).astype(held_as)


def heavy_noise(stream_key, extent, deviation, reach, cuts, heavy, kind=jnp.bfloat16):
    entries = deviation * jax.random.normal(stream_key, extent, jnp.float32)
    if cuts:
        entries = entries * level_of(stream_key, extent, cuts, -0.22, 0.18)
    return jnp.clip(strengthened(entries, jax.random.fold_in(stream_key, 3), *heavy), -reach, reach).astype(kind)


def setup_inputs(seed: int = 0) -> dict:
    splits = jax.random.split(jax.random.key(seed), 8)
    return {
        "q_in": draw_q_in(jax.random.fold_in(splits[7], 71), 0),
        "k_in": draw_k_in(jax.random.fold_in(splits[7], 71), 0),
        "v_in": centred(splits[2], (TOKENS, HD_ALL), 1.0, 6.0, ((0, 512),)),
        "cotangent": heavy_noise(splits[3], (TOKENS, HD_ALL), 0.1, 6.0, ((0, 512),), (0, 1, 512, 6.0)),
        "owner": jax.vmap(lambda own: jax.random.permutation(own, N_SEQ))(jax.random.split(splits[4], N_DP)).reshape((N_DP, N_SEQ)).astype(jnp.int32),
        "gain_q": jnp.clip(1.0 + 0.18 * jax.random.normal(splits[5], (HD_ALL,), jnp.float32), 0.1, 1.9),
        "gain_k": jnp.clip(1.0 + 0.18 * jax.random.normal(splits[6], (HD_ALL,), jnp.float32), 0.1, 1.9),
    }


EPSILON = 1e-06

def rope_tables(positions):
    half_depth = HEAD_DIM // 2
    frequency = 10000.0 ** (-jnp.arange(half_depth, dtype=jnp.float32) / half_depth)
    angles = positions.astype(jnp.float32)[:, None] * frequency[None, :]
    return (jnp.cos(angles)[:, None, :], jnp.sin(angles)[:, None, :])

def rotate(field, cosine_table, sine_table):
    half_depth = field.shape[-1] // 2
    first_half = field[..., :half_depth]
    second_half = field[..., half_depth:]
    return jnp.concatenate([first_half * cosine_table - second_half * sine_table, first_half * sine_table + second_half * cosine_table], axis=-1)

def unrotate(field, cosine_table, sine_table):
    half_depth = field.shape[-1] // 2
    first_half = field[..., :half_depth]
    second_half = field[..., half_depth:]
    return jnp.concatenate([first_half * cosine_table + second_half * sine_table, second_half * cosine_table - first_half * sine_table], axis=-1)

def clip_grads(pieces):
    queries, key_rows, values, upstream = pieces
    factor = HEAD_DIM ** (-0.5)
    scores = jnp.dot(queries, key_rows.T, preferred_element_type=jnp.float32) * factor
    row_max = lax.optimization_barrier(jnp.max(scores, axis=1, keepdims=True))
    lifted = jnp.exp(scores - row_max)
    weights = lifted / lax.optimization_barrier(jnp.sum(lifted, axis=1, keepdims=True))
    slopes = jnp.dot(upstream, values.T, preferred_element_type=jnp.float32)
    center = lax.optimization_barrier(jnp.sum(weights * slopes, axis=1, keepdims=True))
    dscore = (weights * (slopes - center)).astype(jnp.bfloat16)
    dquery = (jnp.dot(dscore, key_rows, preferred_element_type=jnp.float32) * factor).astype(jnp.bfloat16)
    dkey_rows = (jnp.dot(dscore.T, queries, preferred_element_type=jnp.float32) * factor).astype(jnp.bfloat16)
    return (dquery, dkey_rows)

def normalize(raw):
    widened = raw.astype(jnp.float32)
    return widened / jnp.sqrt(lax.optimization_barrier(jnp.mean(widened * widened, axis=1, keepdims=True)) + EPSILON)

def group_grads(item, gain_q, gain_k):
    q_in, k_in, v_in, cotangent, owner = item
    slots = jnp.arange(N_SEQ, dtype=jnp.int32)
    holder = lax.optimization_barrier(jnp.sum(jnp.where(owner[None, :] == slots[:, None], slots[None, :], 0), axis=1)).astype(jnp.int32)

    def by_slot(field):
        return jnp.take(field.reshape(N_SEQ, SPAN_TOK, HD_ALL), holder, axis=0).reshape(GRP_TOK, HD_ALL)
    q_hat = normalize(by_slot(q_in)).reshape(GRP_TOK, HEADS, HEAD_DIM)
    k_hat = normalize(by_slot(k_in)).reshape(GRP_TOK, HEADS, HEAD_DIM)
    positions = jnp.arange(GRP_TOK, dtype=jnp.int32) % CLIP_TOK
    cosine_table, sine_table = rope_tables(positions)
    q_rot = rotate(q_hat * gain_q.reshape(HEADS, HEAD_DIM), cosine_table, sine_table).astype(jnp.bfloat16)
    k_rot = rotate(k_hat * gain_k.reshape(HEADS, HEAD_DIM), cosine_table, sine_table).astype(jnp.bfloat16)
    values = by_slot(v_in).reshape(GRP_TOK, HEADS, HEAD_DIM)
    upstream = by_slot(cotangent).reshape(GRP_TOK, HEADS, HEAD_DIM)

    def per_head(pieces):
        split = tuple((field.reshape(CLIPS_GRP, CLIP_TOK, HEAD_DIM) for field in pieces))
        dquery, dkey_rows = lax.map(clip_grads, split)
        return (dquery.reshape(GRP_TOK, HEAD_DIM), dkey_rows.reshape(GRP_TOK, HEAD_DIM))
    dquery, dkey_rows = lax.map(per_head, tuple((field.transpose(1, 0, 2) for field in (q_rot, k_rot, values, upstream))))
    dquery = lax.optimization_barrier(dquery).astype(jnp.float32).transpose(1, 0, 2)
    dkey_rows = lax.optimization_barrier(dkey_rows).astype(jnp.float32).transpose(1, 0, 2)
    d_qn = unrotate(dquery, cosine_table, sine_table)
    d_kn = unrotate(dkey_rows, cosine_table, sine_table)
    return (lax.optimization_barrier(jnp.sum(d_qn * q_hat, axis=0)).reshape(HD_ALL), lax.optimization_barrier(jnp.sum(d_kn * k_hat, axis=0)).reshape(HD_ALL))

def reference(q_in, k_in, v_in, cotangent, owner, gain_q, gain_k):

    def one_group(item):
        return group_grads(item, gain_q, gain_k)
    shaped = tuple((field.reshape(N_DP, GRP_TOK, HD_ALL) for field in (q_in, k_in, v_in, cotangent)))
    grad_q, grad_k = lax.map(one_group, shaped + (owner,))
    return (lax.optimization_barrier(jnp.sum(grad_q, axis=0)), lax.optimization_barrier(jnp.sum(grad_k, axis=0)))
```

```python
import functools

import jax
import jax.numpy as jnp
import numpy as np
from jax import lax
from jax.experimental import pallas as pl
from jax.experimental.pallas import tpu as pltpu
from jax.sharding import PartitionSpec as P

HEAD_DIM = 128
HALF = HEAD_DIM // 2
SPAN = 128
N_SEQ = 16
N_DP = 32
SPANS_CLIP = 8
CLIP = SPAN * SPANS_CLIP
LOCAL_HEADS = 2
WIDTH = LOCAL_HEADS * HEAD_DIM
HD_ALL = 4096
EPSILON = 1e-06
MESH = pl.DeviceIdType.MESH
FACTOR = HEAD_DIM ** (-0.5)
LOG2E = 1.4426950408889634


def rope_constants():
    frequency = 10000.0 ** (-np.arange(HALF, dtype=np.float64) / HALF)
    angles = frequency[None, :, None] * np.arange(CLIP, dtype=np.float64).reshape(SPANS_CLIP, 1, SPAN)
    return np.cos(angles).astype(np.float32), np.sin(angles).astype(np.float32)


def kernel(
    owner, cos_hbm, sin_hbm, gq_hbm, gk_hbm, q_hbm, k_hbm, v_hbm, c_hbm,
    outq, outk,
    qb, kb, vb, cb, own_rows, stat_out, stat, cosr, sinr, gain_rows, gq, gk,
    krot, kcs, vord, qhat, qrot, probs, acc, red, holder,
    ssem, rsem, stat_ssem, stat_rsem, red_ssem, red_rsem, own_sem, misc_sem,
):
    dp = lax.axis_index("dp")
    me = lax.axis_index("seq")
    x, zh, core = me // 4, (me // 2) % 2, me % 2
    hbm = (q_hbm, k_hbm, v_hbm, c_hbm)
    bufs = (qb, kb, vb, cb)
    Q, K, V, C = range(4)

    def to(k):
        far, dx, dc = k // 8, (k // 2) % 4, k % 2
        return ((x + dx) % 4) * 4 + ((zh + far) % 2) * 2 + (core + dc) % 2

    def source(k):
        far, dx, dc = k // 8, (k // 2) % 4, k % 2
        return ((x + 4 - dx) % 4) * 4 + ((zh + far) % 2) * 2 + (core + dc) % 2

    def send(a, k):
        t = to(k)
        return pltpu.make_async_remote_copy(
            src_ref=hbm[a].at[:, pl.ds(pl.multiple_of(t * WIDTH, WIDTH), WIDTH)],
            dst_ref=bufs[a].at[me],
            send_sem=ssem.at[a, k],
            recv_sem=rsem.at[a, k],
            device_id=(dp, t),
            device_id_type=MESH,
        )

    def arrival(a, k):
        j = source(k)
        return pltpu.make_async_remote_copy(
            src_ref=bufs[a].at[j],
            dst_ref=bufs[a].at[j],
            send_sem=ssem.at[a, k],
            recv_sem=rsem.at[a, k],
            device_id=(dp, j),
            device_id_type=MESH,
        )

    def own_copy(a):
        return pltpu.make_async_copy(
            hbm[a].at[:, pl.ds(pl.multiple_of(me * WIDTH, WIDTH), WIDTH)], bufs[a].at[me], own_sem.at[a]
        )

    def send_stat(k):
        t = to(k)
        return pltpu.make_async_remote_copy(
            src_ref=stat_out,
            dst_ref=stat.at[me],
            send_sem=stat_ssem.at[k],
            recv_sem=stat_rsem.at[k],
            device_id=(dp, t),
            device_id_type=MESH,
        )

    def arrival_stat(k):
        j = source(k)
        return pltpu.make_async_remote_copy(
            src_ref=stat.at[j],
            dst_ref=stat.at[j],
            send_sem=stat_ssem.at[k],
            recv_sem=stat_rsem.at[k],
            device_id=(dp, j),
            device_id_type=MESH,
        )

    def send_acc(i):
        t = (dp + i) % N_DP
        return pltpu.make_async_remote_copy(
            src_ref=acc.at[t],
            dst_ref=red.at[dp],
            send_sem=red_ssem.at[i],
            recv_sem=red_rsem.at[i],
            device_id=(t, me),
            device_id_type=MESH,
        )

    def arrival_acc(i):
        j = (dp + N_DP - i) % N_DP
        return pltpu.make_async_remote_copy(
            src_ref=red.at[j],
            dst_ref=red.at[j],
            send_sem=red_ssem.at[i],
            recv_sem=red_rsem.at[i],
            device_id=(j, me),
            device_id_type=MESH,
        )

    def loop(lo, hi, body):
        def step(i, carry):
            body(i)
            return carry

        lax.fori_loop(lo, hi, step, 0)

    barrier = pltpu.get_barrier_semaphore()
    loop(1, N_SEQ, lambda k: pl.semaphore_signal(barrier, inc=1, device_id=(dp, to(k)), device_id_type=MESH))
    loop(
        1, N_DP,
        lambda i: pl.semaphore_signal(barrier, inc=1, device_id=((dp + i) % N_DP, me), device_id_type=MESH),
    )
    misc = [
        pltpu.make_async_copy(q_hbm, own_rows.at[0], misc_sem.at[0]),
        pltpu.make_async_copy(k_hbm, own_rows.at[1], misc_sem.at[1]),
        pltpu.make_async_copy(cos_hbm, cosr, misc_sem.at[2]),
        pltpu.make_async_copy(sin_hbm, sinr, misc_sem.at[3]),
        pltpu.make_async_copy(gq_hbm, gain_rows.at[0], misc_sem.at[4]),
        pltpu.make_async_copy(gk_hbm, gain_rows.at[1], misc_sem.at[5]),
    ]
    for copy in misc:
        copy.start()
    pl.semaphore_wait(barrier, N_SEQ - 1 + N_DP - 1)

    loop(8, 16, lambda k: send(K, k).start())
    for a in range(4):
        own_copy(a).start()

    for i in range(2):
        misc[i].wait()

        def add(b, total):
            block = own_rows[i, :, pl.ds(pl.multiple_of(b * HEAD_DIM, HEAD_DIM), HEAD_DIM)].astype(jnp.float32)
            return total + block * block

        total = lax.fori_loop(0, HD_ALL // HEAD_DIM, add, jnp.zeros((SPAN, HEAD_DIM), jnp.float32))
        mean = jnp.sum(total.T, axis=0, keepdims=True) * (1.0 / HD_ALL)
        stat_out[i : i + 1, :] = 1.0 / jnp.sqrt(mean + EPSILON)
    stat_out[2:8, :] = jnp.zeros((6, SPAN), jnp.float32)
    loop(1, N_SEQ, lambda k: send_stat(k).start())
    stat[pl.ds(me, 1)] = stat_out[...].reshape(1, 8, SPAN)

    loop(8, 16, lambda k: send(Q, k).start())
    loop(1, 8, lambda k: send(K, k).start())
    loop(1, 8, lambda k: send(Q, k).start())
    loop(8, 16, lambda k: send(V, k).start())
    loop(1, 8, lambda k: send(V, k).start())
    loop(1, 8, lambda k: send(C, k).start())
    loop(8, 16, lambda k: send(C, k).start())

    for s in range(N_SEQ):
        place = jnp.int32(0)
        for j in range(N_SEQ):
            place = jnp.maximum(place, jnp.where(owner[0, j] == s, jnp.int32(j), jnp.int32(0)))
        holder[s] = place
    for copy in misc[2:]:
        copy.wait()
    for h in range(LOCAL_HEADS):
        gq[h] = jnp.broadcast_to(gain_rows[0, h : h + 1, :], (SPAN, HEAD_DIM)).T
        gk[h] = jnp.broadcast_to(gain_rows[1, h : h + 1, :], (SPAN, HEAD_DIM)).T
    acc[...] = jnp.zeros(acc.shape, jnp.float32)
    for a in range(4):
        own_copy(a).wait()

    def wait_key(k):
        arrival_stat(k).wait_recv()
        arrival(K, k).wait_recv()

    loop(1, N_SEQ, wait_key)

    def key_span(s):
        j = holder[s]
        clip, p = s // SPANS_CLIP, s % SPANS_CLIP
        cols = pl.ds(pl.multiple_of(p * SPAN, SPAN), SPAN)
        cs, sn = cosr[p], sinr[p]
        scale = stat[j][1:2, :]
        raw = kb[j]
        for h in range(LOCAL_HEADS):
            hat = raw[:, h * HEAD_DIM : (h + 1) * HEAD_DIM].astype(jnp.float32).T * scale
            lo, hi = hat[:HALF], hat[HALF:]
            lc, hc, ls, hs = lo * cs, hi * cs, lo * sn, hi * sn
            gain = gk[h]
            gl, gh = gain[:HALF], gain[HALF:]
            kcs[h, clip, 0:HALF, cols] = lc.astype(jnp.bfloat16)
            kcs[h, clip, HALF : 2 * HALF, cols] = hc.astype(jnp.bfloat16)
            kcs[h, clip, 2 * HALF : 3 * HALF, cols] = ls.astype(jnp.bfloat16)
            kcs[h, clip, 3 * HALF : 4 * HALF, cols] = hs.astype(jnp.bfloat16)
            rot = jnp.concatenate([gl * lc - gh * hs, gl * ls + gh * hc], axis=0)
            krot[h, clip, cols, :] = rot.T.astype(jnp.bfloat16)

    loop(0, N_SEQ, key_span)

    def query_span(k):
        @pl.when(k > 0)
        def _():
            arrival(Q, k).wait_recv()

        j = source(k)
        slot = owner[0, j]
        clip, p = lax.shift_right_logical(slot, 3), lax.bitwise_and(slot, 7)
        cs, sn = cosr[p], sinr[p]
        scale = stat[j][0:1, :]
        raw = qb[j]
        for h in range(LOCAL_HEADS):
            hat = raw[:, h * HEAD_DIM : (h + 1) * HEAD_DIM].astype(jnp.float32).T * scale
            qhat[k, h] = hat
            scaled = hat * gq[h]
            lo, hi = scaled[:HALF], scaled[HALF:]
            rot = jnp.concatenate([lo * cs - hi * sn, lo * sn + hi * cs], axis=0).astype(jnp.bfloat16)
            qrot[k, h] = rot
            scores = jnp.dot(krot[h, clip], rot, preferred_element_type=jnp.float32)
            peak = jnp.max(scores, axis=0, keepdims=True)
            lifted = jnp.exp2((scores - peak) * (FACTOR * LOG2E))
            probs[k, h] = lifted * (1.0 / jnp.sum(lifted, axis=0, keepdims=True))

    loop(0, N_SEQ, query_span)

    loop(1, N_SEQ, lambda k: arrival(V, k).wait_recv())

    def value_span(s):
        raw = vb[holder[s]]
        rows = pl.ds(pl.multiple_of((s % SPANS_CLIP) * SPAN, SPAN), SPAN)
        for h in range(LOCAL_HEADS):
            vord[h, s // SPANS_CLIP, rows, :] = raw[:, h * HEAD_DIM : (h + 1) * HEAD_DIM]

    loop(0, N_SEQ, value_span)

    def grad_span(k):
        @pl.when(k > 0)
        def _():
            arrival(C, k).wait_recv()

        j = source(k)
        slot = owner[0, j]
        clip, p = lax.shift_right_logical(slot, 3), lax.bitwise_and(slot, 7)
        cs, sn = cosr[p], sinr[p]
        raw = cb[j]
        for h in range(LOCAL_HEADS):
            slopes = lax.dot_general(
                vord[h, clip], raw[:, h * HEAD_DIM : (h + 1) * HEAD_DIM],
                (((1,), (1,)), ((), ())), preferred_element_type=jnp.float32,
            )
            weights = probs[k, h]
            center = jnp.sum(weights * slopes, axis=0, keepdims=True)
            dscore = (weights * (slopes - center)).astype(jnp.bfloat16)
            both = jnp.dot(kcs[h, clip], dscore, preferred_element_type=jnp.float32) * FACTOR
            ul, uh, wl, wh = (both[i * HALF : (i + 1) * HALF] for i in range(4))
            gain = gk[h]
            gl, gh = gain[:HALF], gain[HALF:]
            dl, dh = gl * ul - gh * wh, gl * wl + gh * uh
            hat = qhat[k, h]
            rot = qrot[k, h].astype(jnp.float32)
            ql, qh = rot[:HALF], rot[HALF:]
            gradq = jnp.concatenate([(dl * cs + dh * sn) * hat[:HALF], (dh * cs - dl * sn) * hat[HALF:]], axis=0)
            gradk = jnp.concatenate([ql * ul + qh * wl, qh * uh - ql * wh], axis=0)
            rows = slice(h * 16, (h + 1) * 16)
            acc[rows, 0] += gradq.reshape(16, 8, SPAN)
            acc[rows, 1] += gradk.reshape(16, 8, SPAN)

    loop(0, N_SEQ, grad_span)

    loop(1, N_DP, lambda i: send_acc(i).start())
    red[pl.ds(dp, 1)] = acc[pl.ds(dp, 1)]
    loop(1, N_DP, lambda i: arrival_acc(i).wait_recv())
    total = jnp.sum(red[...], axis=0)
    outq[...] = jnp.sum(total[0].T, axis=0, keepdims=True)
    outk[...] = jnp.sum(total[1].T, axis=0, keepdims=True)

    def wait_sends(k):
        send_stat(k).wait_send()
        for a in range(4):
            send(a, k).wait_send()

    loop(1, N_SEQ, wait_sends)
    loop(1, N_DP, lambda i: send_acc(i).wait_send())


def on_device(cos, sin, q_in, k_in, v_in, cotangent, owner, gain_q, gain_k):
    bf16, f32, dma = jnp.bfloat16, jnp.float32, pltpu.SemaphoreType.DMA
    anywhere = pl.BlockSpec(memory_space=pl.ANY)
    in_vmem = pl.BlockSpec(memory_space=pltpu.VMEM)
    span_buf = pltpu.VMEM((N_SEQ, SPAN, WIDTH), bf16)
    outq, outk = pl.pallas_call(
        kernel,
        out_shape=[jax.ShapeDtypeStruct((1, 8), f32)] * 2,
        in_specs=[pl.BlockSpec(memory_space=pltpu.SMEM)] + [anywhere] * 8,
        out_specs=[in_vmem] * 2,
        scratch_shapes=[
            span_buf, span_buf, span_buf, span_buf,
            pltpu.VMEM((2, SPAN, HD_ALL), bf16),
            pltpu.VMEM((8, SPAN), f32),
            pltpu.VMEM((N_SEQ, 8, SPAN), f32),
            pltpu.VMEM((SPANS_CLIP, HALF, SPAN), f32),
            pltpu.VMEM((SPANS_CLIP, HALF, SPAN), f32),
            pltpu.VMEM((2, LOCAL_HEADS, HEAD_DIM), f32),
            pltpu.VMEM((LOCAL_HEADS, HEAD_DIM, SPAN), f32),
            pltpu.VMEM((LOCAL_HEADS, HEAD_DIM, SPAN), f32),
            pltpu.VMEM((LOCAL_HEADS, 2, CLIP, HEAD_DIM), bf16),
            pltpu.VMEM((LOCAL_HEADS, 2, 2 * HEAD_DIM, CLIP), bf16),
            pltpu.VMEM((LOCAL_HEADS, 2, CLIP, HEAD_DIM), bf16),
            pltpu.VMEM((N_SEQ, LOCAL_HEADS, HEAD_DIM, SPAN), f32),
            pltpu.VMEM((N_SEQ, LOCAL_HEADS, HEAD_DIM, SPAN), bf16),
            pltpu.VMEM((N_SEQ, LOCAL_HEADS, CLIP, SPAN), f32),
            pltpu.VMEM((N_DP, 2, 8, SPAN), f32),
            pltpu.VMEM((N_DP, 2, 8, SPAN), f32),
            pltpu.SMEM((N_SEQ,), jnp.int32),
            dma((4, N_SEQ)), dma((4, N_SEQ)),
            dma((N_SEQ,)), dma((N_SEQ,)),
            dma((N_DP,)), dma((N_DP,)),
            dma((4,)), dma((6,)),
        ],
        compiler_params=pltpu.CompilerParams(
            collective_id=0, has_side_effects=True, vmem_limit_bytes=56 * 2**20
        ),
    )(
        owner, cos, sin, gain_q.reshape(LOCAL_HEADS, HEAD_DIM), gain_k.reshape(LOCAL_HEADS, HEAD_DIM),
        q_in, k_in, v_in, cotangent,
    )
    return outq.reshape(8), outk.reshape(8)


def solution(mesh):
    cos, sin = rope_constants()
    mapped = jax.shard_map(
        on_device,
        mesh=mesh,
        in_specs=(
            P(), P(),
            P(("dp", "seq"), None),
            P(("dp", "seq"), None),
            P(("dp", "seq"), None),
            P(("dp", "seq"), None),
            P("dp", None),
            P("seq"),
            P("seq"),
        ),
        out_specs=(P(("seq", "dp")), P(("seq", "dp"))),
        check_vma=False,
    )
    return lambda *args: mapped(jnp.asarray(cos), jnp.asarray(sin), *args)
```

```python
import functools

import jax
import jax.numpy as jnp
import numpy as np
from jax import lax
from jax.experimental import pallas as pl
from jax.experimental.pallas import tpu as pltpu
from jax.sharding import PartitionSpec as P

HEAD_DIM = 128
HALF = HEAD_DIM // 2
SPAN = 128
N_SEQ = 16
N_DP = 32
SPANS_CLIP = 8
CLIP = SPAN * SPANS_CLIP
LOCAL_HEADS = 2
WIDTH = LOCAL_HEADS * HEAD_DIM
HD_ALL = 4096
EPSILON = 1e-06
MESH = pl.DeviceIdType.MESH
FACTOR = HEAD_DIM ** (-0.5)
LOG2E = 1.4426950408889634
PARTS = [slice(i, i + 256) for i in range(0, CLIP, 256)]


def rope_constants():
    frequency = 10000.0 ** (-np.arange(HALF, dtype=np.float64) / HALF)
    angles = frequency[None, :, None] * np.arange(CLIP, dtype=np.float64).reshape(SPANS_CLIP, 1, SPAN)
    return np.cos(angles).astype(np.float32), np.sin(angles).astype(np.float32)


def kernel(
    owner_hbm, cos_hbm, sin_hbm, gq_hbm, gk_hbm, q_hbm, k_hbm, v_hbm, c_hbm,
    outq, outk,
    qb, kb, vb, cb, own_rows, stat_out, stat, cosr, sinr, gain_rows, gq, gk,
    krot, kcs, vord, qhat, qrot, probs, slopes, acc, sums, red, holder, held, owner,
    ssem, rsem, stat_ssem, stat_rsem, red_ssem, red_rsem, own_sem, misc_sem,
):
    dp = lax.axis_index("dp")
    me = lax.axis_index("seq")
    x, zh, core = me // 4, (me // 2) % 2, me % 2
    hbm = (q_hbm, k_hbm, v_hbm, c_hbm)
    bufs = (qb, kb, vb, cb)
    Q, K, V, C = range(4)

    ahead = [((x + d) % 4) * 4 for d in range(4)]
    halves = [zh * 2, (1 - zh) * 2]
    cores = [core, 1 - core]

    def offset(k):
        return k // 8, (0, 2, 1, 3)[k % 4], (k // 4) % 2

    def to(k):
        far, dx, dc = offset(k)
        return ahead[dx] + halves[far] + cores[dc]

    def source(k):
        far, dx, dc = offset(k)
        return ahead[(4 - dx) % 4] + halves[far] + cores[dc]

    def send(a, k):
        t = to(k)
        return pltpu.make_async_remote_copy(
            src_ref=hbm[a].at[:, pl.ds(pl.multiple_of(t * WIDTH, WIDTH), WIDTH)],
            dst_ref=bufs[a].at[k],
            send_sem=ssem.at[a, k],
            recv_sem=rsem.at[a, k],
            device_id=(dp, t),
            device_id_type=MESH,
        )

    def arrival(a, k):
        return pltpu.make_async_remote_copy(
            src_ref=bufs[a].at[k],
            dst_ref=bufs[a].at[k],
            send_sem=ssem.at[a, k],
            recv_sem=rsem.at[a, k],
            device_id=(dp, me),
            device_id_type=MESH,
        )

    def own_copy(a):
        return pltpu.make_async_copy(
            hbm[a].at[:, pl.ds(pl.multiple_of(me * WIDTH, WIDTH), WIDTH)], bufs[a].at[0], own_sem.at[a]
        )

    def send_stat(k):
        return pltpu.make_async_remote_copy(
            src_ref=stat_out,
            dst_ref=stat.at[k],
            send_sem=stat_ssem.at[k],
            recv_sem=stat_rsem.at[k],
            device_id=(dp, to(k)),
            device_id_type=MESH,
        )

    def arrival_stat(k):
        return pltpu.make_async_remote_copy(
            src_ref=stat.at[k],
            dst_ref=stat.at[k],
            send_sem=stat_ssem.at[k],
            recv_sem=stat_rsem.at[k],
            device_id=(dp, me),
            device_id_type=MESH,
        )

    y, z = dp // 8, dp % 8
    ybits, zbits = ((y // 2) % 2, y % 2), ((z // 4) % 2, (z // 2) % 2, z % 2)

    def flipped(bits, mask):
        total = jnp.int32(0)
        for n, bit in enumerate(bits):
            place = 1 << (len(bits) - 1 - n)
            total = total + ((1 - bit) if mask & place else bit) * place
        return total

    rows_y = [flipped(ybits, m) for m in range(4)]
    parts_z = [flipped(zbits, m) for m in range(8)]

    def partner(i):
        m = 31 - i
        return rows_y[m % 4] * 8 + parts_z[m // 4]

    def send_acc(i):
        return pltpu.make_async_remote_copy(
            src_ref=sums.at[rows_y[(31 - i) % 4]],
            dst_ref=red.at[i],
            send_sem=red_ssem.at[i],
            recv_sem=red_rsem.at[i],
            device_id=(partner(i), me),
            device_id_type=MESH,
        )

    def arrival_acc(i):
        return pltpu.make_async_remote_copy(
            src_ref=red.at[i],
            dst_ref=red.at[i],
            send_sem=red_ssem.at[i],
            recv_sem=red_rsem.at[i],
            device_id=(dp, me),
            device_id_type=MESH,
        )

    def each(lo, hi, body):
        for i in range(lo, hi):
            body(i)

    def loop(lo, hi, body):
        def step(i, carry):
            body(i)
            return carry

        lax.fori_loop(lo, hi, step, 0)

    barrier = pltpu.get_barrier_semaphore()
    each(
        0, N_SEQ - 1,
        lambda i: pl.semaphore_signal(barrier, inc=1, device_id=(dp, to(15 - i)), device_id_type=MESH),
    )
    each(
        0, N_DP - 1,
        lambda i: pl.semaphore_signal(barrier, inc=1, device_id=(partner(i), me), device_id_type=MESH),
    )
    misc = [
        pltpu.make_async_copy(q_hbm, own_rows.at[0], misc_sem.at[0]),
        pltpu.make_async_copy(k_hbm, own_rows.at[1], misc_sem.at[1]),
        pltpu.make_async_copy(cos_hbm, cosr, misc_sem.at[2]),
        pltpu.make_async_copy(sin_hbm, sinr, misc_sem.at[3]),
        pltpu.make_async_copy(gq_hbm, gain_rows.at[0], misc_sem.at[4]),
        pltpu.make_async_copy(gk_hbm, gain_rows.at[1], misc_sem.at[5]),
        pltpu.make_async_copy(owner_hbm, owner, misc_sem.at[6]),
    ]
    for copy in misc:
        copy.start()
    pl.semaphore_wait(barrier, N_SEQ - 1 + N_DP - 1)

    each(8, 16, lambda k: send(K, k).start())
    for a in range(4):
        own_copy(a).start()

    for i in range(2):
        misc[i].wait()

        def add(b, total):
            block = own_rows[i, :, pl.ds(pl.multiple_of(b * HEAD_DIM, HEAD_DIM), HEAD_DIM)].astype(jnp.float32)
            return total + block * block

        total = lax.fori_loop(0, HD_ALL // HEAD_DIM, add, jnp.zeros((SPAN, HEAD_DIM), jnp.float32))
        mean = jnp.sum(total.T, axis=0, keepdims=True) * (1.0 / HD_ALL)
        stat_out[i : i + 1, :] = 1.0 / jnp.sqrt(mean + EPSILON)
    stat_out[2:8, :] = jnp.zeros((6, SPAN), jnp.float32)
    each(1, N_SEQ, lambda k: send_stat(k).start())
    stat[0:1] = stat_out[...].reshape(1, 8, SPAN)

    each(8, 16, lambda k: send(Q, k).start())
    for a in range(4):
        each(1, 8, lambda k: send(a, k).start())
    each(8, 16, lambda k: send(V, k).start())
    each(8, 16, lambda k: send(C, k).start())

    for copy in misc[2:]:
        copy.wait()

    for k in range(N_SEQ):
        held[k] = owner[0, source(k)]

    def find(s):
        place = jnp.int32(0)
        for k in range(N_SEQ):
            place = jnp.maximum(place, jnp.where(held[k] == s, jnp.int32(k), jnp.int32(0)))
        holder[s] = place

    loop(0, N_SEQ, find)
    for h in range(LOCAL_HEADS):
        gq[h] = jnp.broadcast_to(gain_rows[0, h : h + 1, :], (SPAN, HEAD_DIM)).T
        gk[h] = jnp.broadcast_to(gain_rows[1, h : h + 1, :], (SPAN, HEAD_DIM)).T
    acc[...] = jnp.zeros(acc.shape, jnp.float32)
    for a in range(4):
        own_copy(a).wait()

    def wait_key(k):
        arrival_stat(k).wait_recv()
        arrival(K, k).wait_recv()

    each(1, N_SEQ, wait_key)

    def key_span(s):
        j = holder[s]
        clip, p = s // SPANS_CLIP, s % SPANS_CLIP
        cols = pl.ds(pl.multiple_of(p * SPAN, SPAN), SPAN)
        cs, sn = cosr[p], sinr[p]
        scale = stat[j][1:2, :]
        raw = kb[j]
        for h in range(LOCAL_HEADS):
            hat = raw[:, h * HEAD_DIM : (h + 1) * HEAD_DIM].astype(jnp.float32).T * scale
            lo, hi = hat[:HALF], hat[HALF:]
            lc, hc, ls, hs = lo * cs, hi * cs, lo * sn, hi * sn
            gain = gk[h]
            gl, gh = gain[:HALF], gain[HALF:]
            kcs[h, clip, 0:HALF, cols] = lc.astype(jnp.bfloat16)
            kcs[h, clip, HALF : 2 * HALF, cols] = hc.astype(jnp.bfloat16)
            kcs[h, clip, 2 * HALF : 3 * HALF, cols] = ls.astype(jnp.bfloat16)
            kcs[h, clip, 3 * HALF : 4 * HALF, cols] = hs.astype(jnp.bfloat16)
            rot = jnp.concatenate([gl * lc - gh * hs, gl * ls + gh * hc], axis=0)
            krot[h, clip, cols, :] = rot.T.astype(jnp.bfloat16)

    loop(0, N_SEQ, key_span)

    def query_span(k):
        @pl.when(k > 0)
        def _():
            arrival(Q, k).wait_recv()

        slot = held[k]
        clip, p = lax.shift_right_logical(slot, 3), lax.bitwise_and(slot, 7)
        cs, sn = cosr[p], sinr[p]
        scale = stat[k][0:1, :]
        raw = qb[k]
        for h in range(LOCAL_HEADS):
            hat = raw[:, h * HEAD_DIM : (h + 1) * HEAD_DIM].astype(jnp.float32).T * scale
            qhat[k, h] = hat
            scaled = hat * gq[h]
            lo, hi = scaled[:HALF], scaled[HALF:]
            rot = jnp.concatenate([lo * cs - hi * sn, lo * sn + hi * cs], axis=0).astype(jnp.bfloat16)
            qrot[k, h] = rot
            scores = jnp.dot(krot[h, clip], rot, preferred_element_type=jnp.float32)
            peak = jnp.max(scores, axis=0, keepdims=True)
            lifted = jnp.exp2((scores - peak) * (FACTOR * LOG2E))
            probs[k, h] = lifted * (1.0 / jnp.sum(lifted, axis=0, keepdims=True))

    loop(0, N_SEQ, query_span)

    each(1, N_SEQ, lambda k: arrival(V, k).wait_recv())

    def value_span(s):
        raw = vb[holder[s]]
        rows = pl.ds(pl.multiple_of((s % SPANS_CLIP) * SPAN, SPAN), SPAN)
        for h in range(LOCAL_HEADS):
            vord[h, s // SPANS_CLIP, rows, :] = raw[:, h * HEAD_DIM : (h + 1) * HEAD_DIM]

    loop(0, N_SEQ, value_span)

    def grad_span(k):
        @pl.when(k > 0)
        def _():
            arrival(C, k).wait_recv()

        slot = held[k]
        clip, p = lax.shift_right_logical(slot, 3), lax.bitwise_and(slot, 7)
        cs, sn = cosr[p], sinr[p]
        raw = cb[k]
        for h in range(LOCAL_HEADS):
            cotangent = raw[:, h * HEAD_DIM : (h + 1) * HEAD_DIM]
            total = None
            for part in PARTS:
                slopes[h, part] = lax.dot_general(
                    vord[h, clip, part, :], cotangent, (((1,), (1,)), ((), ())), preferred_element_type=jnp.float32
                )
                share = jnp.sum((probs[k, h, part] * slopes[h, part]).reshape(-1, 8, SPAN), axis=0)
                total = share if total is None else total + share
            center = jnp.sum(total, axis=0, keepdims=True)
            both = None
            for part in PARTS:
                dscore = (probs[k, h, part] * (slopes[h, part] - center)).astype(jnp.bfloat16)
                share = jnp.dot(kcs[h, clip, :, part], dscore, preferred_element_type=jnp.float32)
                both = share if both is None else both + share
            both = both * FACTOR
            ul, uh, wl, wh = (both[i * HALF : (i + 1) * HALF] for i in range(4))
            gain = gk[h]
            gl, gh = gain[:HALF], gain[HALF:]
            dl, dh = gl * ul - gh * wh, gl * wl + gh * uh
            hat = qhat[k, h]
            rot = qrot[k, h].astype(jnp.float32)
            ql, qh = rot[:HALF], rot[HALF:]
            acc[2 * h, :HALF] += (dl * cs + dh * sn) * hat[:HALF]
            acc[2 * h, HALF:] += ql * ul + qh * wl
            acc[2 * h + 1, :HALF] += (dh * cs - dl * sn) * hat[HALF:]
            acc[2 * h + 1, HALF:] += qh * uh - ql * wh

    loop(0, N_SEQ, grad_span)

    for i in range(4):
        sums[i] = jnp.sum(acc[i].T, axis=0, keepdims=True)
    each(0, N_DP - 1, lambda i: send_acc(i).start())
    red[N_DP - 1 : N_DP] = sums[pl.ds(y, 1)]

    def wait_sends(k):
        send_stat(k).wait_send()
        for a in range(4):
            send(a, k).wait_send()

    each(1, N_SEQ, wait_sends)
    each(0, N_DP - 1, lambda i: send_acc(i).wait_send())
    each(0, N_DP - 1, lambda i: arrival_acc(i).wait_recv())
    total = jnp.broadcast_to(jnp.sum(red[...], axis=0), (8, SPAN))
    mine = pltpu.roll(total, (SPAN - 8 * z) % SPAN, 1)
    outq[...] = mine[0, 0:8]
    outk[...] = mine[0, HALF : HALF + 8]


def on_device(cos, sin, q_in, k_in, v_in, cotangent, owner, gain_q, gain_k):
    bf16, f32, dma = jnp.bfloat16, jnp.float32, pltpu.SemaphoreType.DMA
    anywhere = pl.BlockSpec(memory_space=pl.ANY)
    in_vmem = pl.BlockSpec(memory_space=pltpu.VMEM)
    span_buf = pltpu.VMEM((N_SEQ, SPAN, WIDTH), bf16)
    outq, outk = pl.pallas_call(
        kernel,
        out_shape=[jax.ShapeDtypeStruct((8,), f32)] * 2,
        in_specs=[anywhere] * 9,
        out_specs=[in_vmem] * 2,
        scratch_shapes=[
            span_buf, span_buf, span_buf, span_buf,
            pltpu.VMEM((2, SPAN, HD_ALL), bf16),
            pltpu.VMEM((8, SPAN), f32),
            pltpu.VMEM((N_SEQ, 8, SPAN), f32),
            pltpu.VMEM((SPANS_CLIP, HALF, SPAN), f32),
            pltpu.VMEM((SPANS_CLIP, HALF, SPAN), f32),
            pltpu.VMEM((2, LOCAL_HEADS, HEAD_DIM), f32),
            pltpu.VMEM((LOCAL_HEADS, HEAD_DIM, SPAN), f32),
            pltpu.VMEM((LOCAL_HEADS, HEAD_DIM, SPAN), f32),
            pltpu.VMEM((LOCAL_HEADS, 2, CLIP, HEAD_DIM), bf16),
            pltpu.VMEM((LOCAL_HEADS, 2, 2 * HEAD_DIM, CLIP), bf16),
            pltpu.VMEM((LOCAL_HEADS, 2, CLIP, HEAD_DIM), bf16),
            pltpu.VMEM((N_SEQ, LOCAL_HEADS, HEAD_DIM, SPAN), f32),
            pltpu.VMEM((N_SEQ, LOCAL_HEADS, HEAD_DIM, SPAN), bf16),
            pltpu.VMEM((N_SEQ, LOCAL_HEADS, CLIP, SPAN), f32),
            pltpu.VMEM((LOCAL_HEADS, CLIP, SPAN), f32),
            pltpu.VMEM((4, SPAN, SPAN), f32),
            pltpu.VMEM((4, 1, SPAN), f32),
            pltpu.VMEM((N_DP, 1, SPAN), f32),
            pltpu.SMEM((N_SEQ,), jnp.int32),
            pltpu.SMEM((N_SEQ,), jnp.int32),
            pltpu.SMEM((1, N_SEQ), jnp.int32),
            dma((4, N_SEQ)), dma((4, N_SEQ)),
            dma((N_SEQ,)), dma((N_SEQ,)),
            dma((N_DP,)), dma((N_DP,)),
            dma((4,)), dma((7,)),
        ],
        compiler_params=pltpu.CompilerParams(
            collective_id=0, has_side_effects=True, vmem_limit_bytes=56 * 2**20
        ),
    )(
        owner, cos, sin, gain_q.reshape(LOCAL_HEADS, HEAD_DIM), gain_k.reshape(LOCAL_HEADS, HEAD_DIM),
        q_in, k_in, v_in, cotangent,
    )
    return outq, outk


def solution(mesh):
    cos, sin = rope_constants()
    mapped = jax.shard_map(
        on_device,
        mesh=mesh,
        in_specs=(
            P(), P(),
            P(("dp", "seq"), None),
            P(("dp", "seq"), None),
            P(("dp", "seq"), None),
            P(("dp", "seq"), None),
            P("dp", None),
            P("seq"),
            P("seq"),
        ),
        out_specs=(P(("seq", "dp")), P(("seq", "dp"))),
        check_vma=False,
    )
    return lambda *args: mapped(jnp.asarray(cos), jnp.asarray(sin), *args)
```

```python
import functools

import jax
import jax.numpy as jnp
import numpy as np
from jax import lax
from jax.experimental import pallas as pl
from jax.experimental.pallas import tpu as pltpu
from jax.sharding import PartitionSpec as P

HEAD_DIM = 128
HALF = HEAD_DIM // 2
SPAN = 128
N_SEQ = 16
N_DP = 32
SPANS_CLIP = 8
CLIP = SPAN * SPANS_CLIP
LOCAL_HEADS = 2
WIDTH = LOCAL_HEADS * HEAD_DIM
HD_ALL = 4096
EPSILON = 1e-06
MESH = pl.DeviceIdType.MESH
FACTOR = HEAD_DIM ** (-0.5)
LOG2E = 1.4426950408889634
PARTS = [slice(i, i + 256) for i in range(0, CLIP, 256)]


def rope_constants():
    frequency = 10000.0 ** (-np.arange(HALF, dtype=np.float64) / HALF)
    angles = frequency[None, :, None] * np.arange(CLIP, dtype=np.float64).reshape(SPANS_CLIP, 1, SPAN)
    return np.cos(angles).astype(np.float32), np.sin(angles).astype(np.float32)


def kernel(
    owner_hbm, cos_hbm, sin_hbm, gq_hbm, gk_hbm, q_hbm, k_hbm, v_hbm, c_hbm,
    out,
    qb, kb, vb, cb, own_rows, stat_out, stat, cosr, sinr, gain_rows, gq, gk,
    krot, kcs, vord, qhat, qrot, probs, slopes, acc, sums, red, holder, held, owner,
    ssem, rsem, stat_ssem, stat_rsem, red_ssem, red_rsem, own_sem, misc_sem,
):
    dp = lax.axis_index("dp")
    me = lax.axis_index("seq")
    x, zh, core = me // 4, (me // 2) % 2, me % 2
    hbm = (q_hbm, k_hbm, v_hbm, c_hbm)
    bufs = (qb, kb, vb, cb)
    Q, K, V, C = range(4)

    ahead = [((x + d) % 4) * 4 for d in range(4)]
    halves = [zh * 2, (1 - zh) * 2]
    cores = [core, 1 - core]

    def offset(k):
        return k // 8, (0, 2, 1, 3)[k % 4], (k // 4) % 2

    def to(k):
        far, dx, dc = offset(k)
        return ahead[dx] + halves[far] + cores[dc]

    def source(k):
        far, dx, dc = offset(k)
        return ahead[(4 - dx) % 4] + halves[far] + cores[dc]

    def send(a, k):
        t = to(k)
        return pltpu.make_async_remote_copy(
            src_ref=hbm[a].at[:, pl.ds(pl.multiple_of(t * WIDTH, WIDTH), WIDTH)],
            dst_ref=bufs[a].at[k],
            send_sem=ssem.at[a, k],
            recv_sem=rsem.at[a, k],
            device_id=(dp, t),
            device_id_type=MESH,
        )

    def arrival(a, k):
        return pltpu.make_async_remote_copy(
            src_ref=bufs[a].at[k],
            dst_ref=bufs[a].at[k],
            send_sem=ssem.at[a, k],
            recv_sem=rsem.at[a, k],
            device_id=(dp, me),
            device_id_type=MESH,
        )

    def own_copy(a):
        return pltpu.make_async_copy(
            hbm[a].at[:, pl.ds(pl.multiple_of(me * WIDTH, WIDTH), WIDTH)], bufs[a].at[0], own_sem.at[a]
        )

    def send_stat(k):
        return pltpu.make_async_remote_copy(
            src_ref=stat_out,
            dst_ref=stat.at[k],
            send_sem=stat_ssem.at[k],
            recv_sem=stat_rsem.at[k],
            device_id=(dp, to(k)),
            device_id_type=MESH,
        )

    def arrival_stat(k):
        return pltpu.make_async_remote_copy(
            src_ref=stat.at[k],
            dst_ref=stat.at[k],
            send_sem=stat_ssem.at[k],
            recv_sem=stat_rsem.at[k],
            device_id=(dp, me),
            device_id_type=MESH,
        )

    y, z = dp // 8, dp % 8
    ybits, zbits = ((y // 2) % 2, y % 2), ((z // 4) % 2, (z // 2) % 2, z % 2)

    def flipped(bits, mask):
        total = jnp.int32(0)
        for n, bit in enumerate(bits):
            place = 1 << (len(bits) - 1 - n)
            total = total + ((1 - bit) if mask & place else bit) * place
        return total

    rows_y = [flipped(ybits, m) for m in range(4)]
    parts_z = [flipped(zbits, m) for m in range(8)]

    def partner(i):
        m = 31 - i
        return rows_y[m % 4] * 8 + parts_z[m // 4]

    def send_acc(i):
        return pltpu.make_async_remote_copy(
            src_ref=sums.at[rows_y[(31 - i) % 4]],
            dst_ref=red.at[i],
            send_sem=red_ssem.at[i],
            recv_sem=red_rsem.at[i],
            device_id=(partner(i), me),
            device_id_type=MESH,
        )

    def arrival_acc(i):
        return pltpu.make_async_remote_copy(
            src_ref=red.at[i],
            dst_ref=red.at[i],
            send_sem=red_ssem.at[i],
            recv_sem=red_rsem.at[i],
            device_id=(dp, me),
            device_id_type=MESH,
        )

    def each(lo, hi, body):
        for i in range(lo, hi):
            body(i)

    def loop(lo, hi, body):
        def step(i, carry):
            body(i)
            return carry

        lax.fori_loop(lo, hi, step, 0)

    barrier = pltpu.get_barrier_semaphore()
    each(
        0, N_SEQ - 1,
        lambda i: pl.semaphore_signal(barrier, inc=1, device_id=(dp, to(15 - i)), device_id_type=MESH),
    )
    each(
        0, N_DP - 1,
        lambda i: pl.semaphore_signal(barrier, inc=1, device_id=(partner(i), me), device_id_type=MESH),
    )
    misc = [
        pltpu.make_async_copy(q_hbm, own_rows.at[0], misc_sem.at[0]),
        pltpu.make_async_copy(k_hbm, own_rows.at[1], misc_sem.at[1]),
        pltpu.make_async_copy(cos_hbm, cosr, misc_sem.at[2]),
        pltpu.make_async_copy(sin_hbm, sinr, misc_sem.at[3]),
        pltpu.make_async_copy(gq_hbm, gain_rows.at[0], misc_sem.at[4]),
        pltpu.make_async_copy(gk_hbm, gain_rows.at[1], misc_sem.at[5]),
        pltpu.make_async_copy(owner_hbm, owner, misc_sem.at[6]),
    ]
    for copy in misc:
        copy.start()
    pl.semaphore_wait(barrier, N_SEQ - 1 + N_DP - 1)

    each(8, 16, lambda k: send(K, k).start())
    for a in range(4):
        own_copy(a).start()

    for i in range(2):
        misc[i].wait()

        def add(b, total):
            block = own_rows[i, :, pl.ds(pl.multiple_of(b * HEAD_DIM, HEAD_DIM), HEAD_DIM)].astype(jnp.float32)
            return total + block * block

        total = lax.fori_loop(0, HD_ALL // HEAD_DIM, add, jnp.zeros((SPAN, HEAD_DIM), jnp.float32))
        mean = jnp.sum(total.T, axis=0, keepdims=True) * (1.0 / HD_ALL)
        stat_out[i : i + 1, :] = 1.0 / jnp.sqrt(mean + EPSILON)
    each(1, N_SEQ, lambda k: send_stat(k).start())
    stat[0:1] = stat_out[...].reshape(1, 2, SPAN)

    each(8, 16, lambda k: send(V, k).start())
    each(8, 16, lambda k: send(Q, k).start())
    for a in range(4):
        each(1, 8, lambda k: send(a, k).start())
    each(8, 16, lambda k: send(C, k).start())

    for copy in misc[2:]:
        copy.wait()

    for k in range(N_SEQ):
        held[k] = owner[0, source(k)]

    def find(s):
        place = jnp.int32(0)
        for k in range(N_SEQ):
            place = jnp.maximum(place, jnp.where(held[k] == s, jnp.int32(k), jnp.int32(0)))
        holder[s] = place

    loop(0, N_SEQ, find)
    for h in range(LOCAL_HEADS):
        gq[h] = jnp.broadcast_to(gain_rows[0, h : h + 1, :], (SPAN, HEAD_DIM)).T
        gk[h] = jnp.broadcast_to(gain_rows[1, h : h + 1, :], (SPAN, HEAD_DIM)).T
    acc[...] = jnp.zeros(acc.shape, jnp.float32)
    for a in range(4):
        own_copy(a).wait()

    def wait_key(k):
        arrival_stat(k).wait_recv()
        arrival(K, k).wait_recv()

    each(1, N_SEQ, wait_key)

    def key_span(s):
        j = holder[s]
        clip, p = s // SPANS_CLIP, s % SPANS_CLIP
        cols = pl.ds(pl.multiple_of(p * SPAN, SPAN), SPAN)
        cs, sn = cosr[p], sinr[p]
        scale = stat[j][1:2, :]
        raw = kb[j]
        for h in range(LOCAL_HEADS):
            hat = raw[:, h * HEAD_DIM : (h + 1) * HEAD_DIM].astype(jnp.float32).T * scale
            lo, hi = hat[:HALF], hat[HALF:]
            lc, hc, ls, hs = lo * cs, hi * cs, lo * sn, hi * sn
            gain = gk[h]
            gl, gh = gain[:HALF], gain[HALF:]
            kcs[h, clip, 0:HALF, cols] = lc.astype(jnp.bfloat16)
            kcs[h, clip, HALF : 2 * HALF, cols] = hc.astype(jnp.bfloat16)
            kcs[h, clip, 2 * HALF : 3 * HALF, cols] = ls.astype(jnp.bfloat16)
            kcs[h, clip, 3 * HALF : 4 * HALF, cols] = hs.astype(jnp.bfloat16)
            rot = jnp.concatenate([gl * lc - gh * hs, gl * ls + gh * hc], axis=0)
            krot[h, clip, cols, :] = rot.T.astype(jnp.bfloat16)

    loop(0, N_SEQ, key_span)

    def query_span(k):
        slot = held[k]
        clip, p = lax.shift_right_logical(slot, 3), lax.bitwise_and(slot, 7)
        cs, sn = cosr[p], sinr[p]
        scale = stat[k][0:1, :]
        raw = qb[k]
        for h in range(LOCAL_HEADS):
            hat = raw[:, h * HEAD_DIM : (h + 1) * HEAD_DIM].astype(jnp.float32).T * scale
            qhat[k, h] = hat
            scaled = hat * gq[h]
            lo, hi = scaled[:HALF], scaled[HALF:]
            rot = jnp.concatenate([lo * cs - hi * sn, lo * sn + hi * cs], axis=0).astype(jnp.bfloat16)
            qrot[k, h] = rot
            scores = jnp.dot(krot[h, clip], rot, preferred_element_type=jnp.float32)
            peak = jnp.max(scores, axis=0, keepdims=True)
            lifted = jnp.exp2((scores - peak) * (FACTOR * LOG2E))
            probs[k, h] = lifted * (1.0 / jnp.sum(lifted, axis=0, keepdims=True))

    each(1, 8, lambda k: arrival(Q, k).wait_recv())
    loop(0, 8, query_span)

    each(1, N_SEQ, lambda k: arrival(V, k).wait_recv())

    def value_span(s):
        raw = vb[holder[s]]
        rows = pl.ds(pl.multiple_of((s % SPANS_CLIP) * SPAN, SPAN), SPAN)
        for h in range(LOCAL_HEADS):
            vord[h, s // SPANS_CLIP, rows, :] = raw[:, h * HEAD_DIM : (h + 1) * HEAD_DIM]

    loop(0, N_SEQ, value_span)

    def grad_span(k):
        slot = held[k]
        clip, p = lax.shift_right_logical(slot, 3), lax.bitwise_and(slot, 7)
        cs, sn = cosr[p], sinr[p]
        raw = cb[k]
        for h in range(LOCAL_HEADS):
            cotangent = raw[:, h * HEAD_DIM : (h + 1) * HEAD_DIM]
            total = None
            for part in PARTS:
                slopes[h, part] = lax.dot_general(
                    vord[h, clip, part, :], cotangent, (((1,), (1,)), ((), ())), preferred_element_type=jnp.float32
                )
                share = jnp.sum((probs[k, h, part] * slopes[h, part]).reshape(-1, 8, SPAN), axis=0)
                total = share if total is None else total + share
            center = jnp.sum(total, axis=0, keepdims=True)
            both = None
            for part in PARTS:
                dscore = (probs[k, h, part] * (slopes[h, part] - center)).astype(jnp.bfloat16)
                share = jnp.dot(kcs[h, clip, :, part], dscore, preferred_element_type=jnp.float32)
                both = share if both is None else both + share
            both = both * FACTOR
            ul, uh, wl, wh = (both[i * HALF : (i + 1) * HALF] for i in range(4))
            gain = gk[h]
            gl, gh = gain[:HALF], gain[HALF:]
            dl, dh = gl * ul - gh * wh, gl * wl + gh * uh
            hat = qhat[k, h]
            rot = qrot[k, h].astype(jnp.float32)
            ql, qh = rot[:HALF], rot[HALF:]
            acc[2 * h, :HALF] += (dl * cs + dh * sn) * hat[:HALF]
            acc[2 * h, HALF:] += ql * ul + qh * wl
            acc[2 * h + 1, :HALF] += (dh * cs - dl * sn) * hat[HALF:]
            acc[2 * h + 1, HALF:] += qh * uh - ql * wh

    each(1, 8, lambda k: arrival(C, k).wait_recv())
    loop(0, 8, grad_span)

    def far_query(k):
        arrival(Q, k).wait_recv()
        query_span(k)

    loop(8, N_SEQ, far_query)

    def far_grad(k):
        arrival(C, k).wait_recv()
        grad_span(k)

    loop(8, N_SEQ, far_grad)

    for i in range(4):
        sums[i] = jnp.sum(acc[i].T, axis=0, keepdims=True)
    each(0, N_DP - 1, lambda i: send_acc(i).start())
    red[N_DP - 1 : N_DP] = sums[pl.ds(y, 1)]

    def wait_sends(k):
        send_stat(k).wait_send()
        for a in range(4):
            send(a, k).wait_send()

    each(1, N_SEQ, wait_sends)
    each(0, N_DP - 1, lambda i: send_acc(i).wait_send())
    each(0, N_DP - 1, lambda i: arrival_acc(i).wait_recv())
    total = jnp.broadcast_to(jnp.sum(red[...], axis=0), (8, SPAN))
    mine = pltpu.roll(total, (SPAN - 8 * z) % SPAN, 1)
    out[...] = mine[0:1]


def on_device(cos, sin, q_in, k_in, v_in, cotangent, owner, gain_q, gain_k):
    bf16, f32, dma = jnp.bfloat16, jnp.float32, pltpu.SemaphoreType.DMA
    anywhere = pl.BlockSpec(memory_space=pl.ANY)
    in_vmem = pl.BlockSpec(memory_space=pltpu.VMEM)
    span_buf = pltpu.VMEM((N_SEQ, SPAN, WIDTH), bf16)
    out = pl.pallas_call(
        kernel,
        out_shape=jax.ShapeDtypeStruct((1, SPAN), f32),
        in_specs=[anywhere] * 9,
        out_specs=in_vmem,
        scratch_shapes=[
            span_buf, span_buf, span_buf, span_buf,
            pltpu.VMEM((2, SPAN, HD_ALL), bf16),
            pltpu.VMEM((2, SPAN), f32),
            pltpu.VMEM((N_SEQ, 2, SPAN), f32),
            pltpu.VMEM((SPANS_CLIP, HALF, SPAN), f32),
            pltpu.VMEM((SPANS_CLIP, HALF, SPAN), f32),
            pltpu.VMEM((2, LOCAL_HEADS, HEAD_DIM), f32),
            pltpu.VMEM((LOCAL_HEADS, HEAD_DIM, SPAN), f32),
            pltpu.VMEM((LOCAL_HEADS, HEAD_DIM, SPAN), f32),
            pltpu.VMEM((LOCAL_HEADS, 2, CLIP, HEAD_DIM), bf16),
            pltpu.VMEM((LOCAL_HEADS, 2, 2 * HEAD_DIM, CLIP), bf16),
            pltpu.VMEM((LOCAL_HEADS, 2, CLIP, HEAD_DIM), bf16),
            pltpu.VMEM((N_SEQ, LOCAL_HEADS, HEAD_DIM, SPAN), f32),
            pltpu.VMEM((N_SEQ, LOCAL_HEADS, HEAD_DIM, SPAN), bf16),
            pltpu.VMEM((N_SEQ, LOCAL_HEADS, CLIP, SPAN), f32),
            pltpu.VMEM((LOCAL_HEADS, CLIP, SPAN), f32),
            pltpu.VMEM((4, SPAN, SPAN), f32),
            pltpu.VMEM((4, 1, SPAN), f32),
            pltpu.VMEM((N_DP, 1, SPAN), f32),
            pltpu.SMEM((N_SEQ,), jnp.int32),
            pltpu.SMEM((N_SEQ,), jnp.int32),
            pltpu.SMEM((1, N_SEQ), jnp.int32),
            dma((4, N_SEQ)), dma((4, N_SEQ)),
            dma((N_SEQ,)), dma((N_SEQ,)),
            dma((N_DP,)), dma((N_DP,)),
            dma((4,)), dma((7,)),
        ],
        compiler_params=pltpu.CompilerParams(
            collective_id=0, has_side_effects=True, vmem_limit_bytes=56 * 2**20
        ),
    )(
        owner, cos, sin, gain_q.reshape(LOCAL_HEADS, HEAD_DIM), gain_k.reshape(LOCAL_HEADS, HEAD_DIM),
        q_in, k_in, v_in, cotangent,
    )
    return out[0, 0:8], out[0, HALF : HALF + 8]


def solution(mesh):
    cos, sin = rope_constants()
    mapped = jax.shard_map(
        on_device,
        mesh=mesh,
        in_specs=(
            P(), P(),
            P(("dp", "seq"), None),
            P(("dp", "seq"), None),
            P(("dp", "seq"), None),
            P(("dp", "seq"), None),
            P("dp", None),
            P("seq"),
            P("seq"),
        ),
        out_specs=(P(("seq", "dp")), P(("seq", "dp"))),
        check_vma=False,
    )
    return lambda *args: mapped(jnp.asarray(cos), jnp.asarray(sin), *args)
```

```python
import functools

import jax
import jax.numpy as jnp
import numpy as np
from jax import lax
from jax.experimental import pallas as pl
from jax.experimental.pallas import tpu as pltpu
from jax.sharding import PartitionSpec as P

HEAD_DIM = 128
HALF = HEAD_DIM // 2
SPAN = 128
N_SEQ = 16
N_DP = 32
SPANS_CLIP = 8
CLIP = SPAN * SPANS_CLIP
LOCAL_HEADS = 2
WIDTH = LOCAL_HEADS * HEAD_DIM
HD_ALL = 4096
EPSILON = 1e-06
MESH = pl.DeviceIdType.MESH
FACTOR = HEAD_DIM ** (-0.5)
LOG2E = 1.4426950408889634
PARTS = [slice(i, i + 256) for i in range(0, CLIP, 256)]


def rope_constants():
    frequency = 10000.0 ** (-np.arange(HALF, dtype=np.float64) / HALF)
    angles = frequency[None, :, None] * np.arange(CLIP, dtype=np.float64).reshape(SPANS_CLIP, 1, SPAN)
    return np.cos(angles).astype(np.float32), np.sin(angles).astype(np.float32)


def kernel(
    owner_hbm, cos_hbm, sin_hbm, gq_hbm, gk_hbm, q_hbm, k_hbm, v_hbm, c_hbm,
    out,
    qb, kb, vb, cb, own_rows, stat_out, stat, cosr, sinr, gain_rows, gq, gk,
    krot, kcs, vord, qhat, qrot, probs, slopes, acc, sums, red, holder, held, owner,
    ssem, rsem, stat_ssem, stat_rsem, red_ssem, red_rsem, own_sem, misc_sem,
):
    dp = lax.axis_index("dp")
    me = lax.axis_index("seq")
    x, zh, core = me // 4, (me // 2) % 2, me % 2
    hbm = (q_hbm, k_hbm, v_hbm, c_hbm)
    bufs = (qb, kb, vb, cb)
    Q, K, V, C = range(4)

    ahead = [((x + d) % 4) * 4 for d in range(4)]
    halves = [zh * 2, (1 - zh) * 2]
    cores = [core, 1 - core]

    def offset(k):
        return k // 8, (2, 3, 1, 0)[k % 4] if k >= 8 else (0, 2, 1, 3)[k % 4], (k // 4) % 2

    def to(k):
        far, dx, dc = offset(k)
        return ahead[dx] + halves[far] + cores[dc]

    def source(k):
        far, dx, dc = offset(k)
        return ahead[(4 - dx) % 4] + halves[far] + cores[dc]

    def send(a, k):
        t = to(k)
        return pltpu.make_async_remote_copy(
            src_ref=hbm[a].at[:, pl.ds(pl.multiple_of(t * WIDTH, WIDTH), WIDTH)],
            dst_ref=bufs[a].at[k],
            send_sem=ssem.at[a, k],
            recv_sem=rsem.at[a, k],
            device_id=(dp, t),
            device_id_type=MESH,
        )

    def arrival(a, k):
        return pltpu.make_async_remote_copy(
            src_ref=bufs[a].at[k],
            dst_ref=bufs[a].at[k],
            send_sem=ssem.at[a, k],
            recv_sem=rsem.at[a, k],
            device_id=(dp, me),
            device_id_type=MESH,
        )

    def own_copy(a):
        return pltpu.make_async_copy(
            hbm[a].at[:, pl.ds(pl.multiple_of(me * WIDTH, WIDTH), WIDTH)], bufs[a].at[0], own_sem.at[a]
        )

    def send_stat(k):
        return pltpu.make_async_remote_copy(
            src_ref=stat_out,
            dst_ref=stat.at[k],
            send_sem=stat_ssem.at[k],
            recv_sem=stat_rsem.at[k],
            device_id=(dp, to(k)),
            device_id_type=MESH,
        )

    def arrival_stat(k):
        return pltpu.make_async_remote_copy(
            src_ref=stat.at[k],
            dst_ref=stat.at[k],
            send_sem=stat_ssem.at[k],
            recv_sem=stat_rsem.at[k],
            device_id=(dp, me),
            device_id_type=MESH,
        )

    y, z = dp // 8, dp % 8
    ybits, zbits = ((y // 2) % 2, y % 2), ((z // 4) % 2, (z // 2) % 2, z % 2)

    def flipped(bits, mask):
        total = jnp.int32(0)
        for n, bit in enumerate(bits):
            place = 1 << (len(bits) - 1 - n)
            total = total + ((1 - bit) if mask & place else bit) * place
        return total

    rows_y = [flipped(ybits, m) for m in range(4)]
    parts_z = [flipped(zbits, m) for m in range(8)]

    def partner(i):
        m = 31 - i
        return rows_y[m % 4] * 8 + parts_z[m // 4]

    def send_acc(i):
        return pltpu.make_async_remote_copy(
            src_ref=sums.at[rows_y[(31 - i) % 4]],
            dst_ref=red.at[i],
            send_sem=red_ssem.at[i],
            recv_sem=red_rsem.at[i],
            device_id=(partner(i), me),
            device_id_type=MESH,
        )

    def arrival_acc(i):
        return pltpu.make_async_remote_copy(
            src_ref=red.at[i],
            dst_ref=red.at[i],
            send_sem=red_ssem.at[i],
            recv_sem=red_rsem.at[i],
            device_id=(dp, me),
            device_id_type=MESH,
        )

    def each(lo, hi, body):
        for i in range(lo, hi):
            body(i)

    def loop(lo, hi, body):
        def step(i, carry):
            body(i)
            return carry

        lax.fori_loop(lo, hi, step, 0)

    barrier = pltpu.get_barrier_semaphore()
    each(
        0, N_SEQ - 1,
        lambda i: pl.semaphore_signal(barrier, inc=1, device_id=(dp, to(15 - i)), device_id_type=MESH),
    )
    each(
        0, N_DP - 1,
        lambda i: pl.semaphore_signal(barrier, inc=1, device_id=(partner(i), me), device_id_type=MESH),
    )
    misc = [
        pltpu.make_async_copy(q_hbm, own_rows.at[0], misc_sem.at[0]),
        pltpu.make_async_copy(k_hbm, own_rows.at[1], misc_sem.at[1]),
        pltpu.make_async_copy(cos_hbm, cosr, misc_sem.at[2]),
        pltpu.make_async_copy(sin_hbm, sinr, misc_sem.at[3]),
        pltpu.make_async_copy(gq_hbm, gain_rows.at[0], misc_sem.at[4]),
        pltpu.make_async_copy(gk_hbm, gain_rows.at[1], misc_sem.at[5]),
        pltpu.make_async_copy(owner_hbm, owner, misc_sem.at[6]),
    ]
    for copy in misc:
        copy.start()
    pl.semaphore_wait(barrier, N_SEQ - 1 + N_DP - 1)

    each(8, 16, lambda k: send(K, k).start())
    for a in range(4):
        own_copy(a).start()

    for i in range(2):
        misc[i].wait()

        def add(b, total):
            block = own_rows[i, :, pl.ds(pl.multiple_of(b * HEAD_DIM, HEAD_DIM), HEAD_DIM)].astype(jnp.float32)
            return total + block * block

        total = lax.fori_loop(0, HD_ALL // HEAD_DIM, add, jnp.zeros((SPAN, HEAD_DIM), jnp.float32))
        mean = jnp.sum(total.T, axis=0, keepdims=True) * (1.0 / HD_ALL)
        stat_out[i : i + 1, :] = 1.0 / jnp.sqrt(mean + EPSILON)
    each(1, N_SEQ, lambda k: send_stat(k).start())
    stat[0:1] = stat_out[...].reshape(1, 2, SPAN)

    each(8, 16, lambda k: send(V, k).start())
    each(8, 16, lambda k: send(Q, k).start())
    for a in range(4):
        each(1, 8, lambda k: send(a, k).start())
    each(8, 16, lambda k: send(C, k).start())

    for copy in misc[2:]:
        copy.wait()

    for k in range(N_SEQ):
        held[k] = owner[0, source(k)]

    def find(s):
        place = jnp.int32(0)
        for k in range(N_SEQ):
            place = jnp.maximum(place, jnp.where(held[k] == s, jnp.int32(k), jnp.int32(0)))
        holder[s] = place

    loop(0, N_SEQ, find)
    for h in range(LOCAL_HEADS):
        gq[h] = jnp.broadcast_to(gain_rows[0, h : h + 1, :], (SPAN, HEAD_DIM)).T
        gk[h] = jnp.broadcast_to(gain_rows[1, h : h + 1, :], (SPAN, HEAD_DIM)).T
    acc[...] = jnp.zeros(acc.shape, jnp.float32)
    for a in range(4):
        own_copy(a).wait()

    def wait_key(k):
        arrival_stat(k).wait_recv()
        arrival(K, k).wait_recv()

    each(1, N_SEQ, wait_key)

    def key_span(s):
        j = holder[s]
        clip, p = s // SPANS_CLIP, s % SPANS_CLIP
        cols = pl.ds(pl.multiple_of(p * SPAN, SPAN), SPAN)
        cs, sn = cosr[p], sinr[p]
        scale = stat[j][1:2, :]
        raw = kb[j]
        for h in range(LOCAL_HEADS):
            hat = raw[:, h * HEAD_DIM : (h + 1) * HEAD_DIM].astype(jnp.float32).T * scale
            lo, hi = hat[:HALF], hat[HALF:]
            lc, hc, ls, hs = lo * cs, hi * cs, lo * sn, hi * sn
            gain = gk[h]
            gl, gh = gain[:HALF], gain[HALF:]
            kcs[h, clip, 0:HALF, cols] = lc.astype(jnp.bfloat16)
            kcs[h, clip, HALF : 2 * HALF, cols] = hc.astype(jnp.bfloat16)
            kcs[h, clip, 2 * HALF : 3 * HALF, cols] = ls.astype(jnp.bfloat16)
            kcs[h, clip, 3 * HALF : 4 * HALF, cols] = hs.astype(jnp.bfloat16)
            rot = jnp.concatenate([gl * lc - gh * hs, gl * ls + gh * hc], axis=0)
            krot[h, clip, cols, :] = rot.T.astype(jnp.bfloat16)

    loop(0, N_SEQ, key_span)

    def query_span(k):
        slot = held[k]
        clip, p = lax.shift_right_logical(slot, 3), lax.bitwise_and(slot, 7)
        cs, sn = cosr[p], sinr[p]
        scale = stat[k][0:1, :]
        raw = qb[k]
        for h in range(LOCAL_HEADS):
            hat = raw[:, h * HEAD_DIM : (h + 1) * HEAD_DIM].astype(jnp.float32).T * scale
            qhat[k, h] = hat
            scaled = hat * gq[h]
            lo, hi = scaled[:HALF], scaled[HALF:]
            rot = jnp.concatenate([lo * cs - hi * sn, lo * sn + hi * cs], axis=0).astype(jnp.bfloat16)
            qrot[k, h] = rot
            scores = jnp.dot(krot[h, clip], rot, preferred_element_type=jnp.float32)
            peak = jnp.max(scores, axis=0, keepdims=True)
            lifted = jnp.exp2((scores - peak) * (FACTOR * LOG2E))
            probs[k, h] = lifted * (1.0 / jnp.sum(lifted, axis=0, keepdims=True))

    each(1, 8, lambda k: arrival(Q, k).wait_recv())
    loop(0, 8, query_span)

    each(1, N_SEQ, lambda k: arrival(V, k).wait_recv())

    def value_span(s):
        raw = vb[holder[s]]
        rows = pl.ds(pl.multiple_of((s % SPANS_CLIP) * SPAN, SPAN), SPAN)
        for h in range(LOCAL_HEADS):
            vord[h, s // SPANS_CLIP, rows, :] = raw[:, h * HEAD_DIM : (h + 1) * HEAD_DIM]

    loop(0, N_SEQ, value_span)

    def grad_span(k):
        slot = held[k]
        clip, p = lax.shift_right_logical(slot, 3), lax.bitwise_and(slot, 7)
        cs, sn = cosr[p], sinr[p]
        raw = cb[k]
        for h in range(LOCAL_HEADS):
            cotangent = raw[:, h * HEAD_DIM : (h + 1) * HEAD_DIM]
            total = None
            for part in PARTS:
                slopes[h, part] = lax.dot_general(
                    vord[h, clip, part, :], cotangent, (((1,), (1,)), ((), ())), preferred_element_type=jnp.float32
                )
                share = jnp.sum((probs[k, h, part] * slopes[h, part]).reshape(-1, 8, SPAN), axis=0)
                total = share if total is None else total + share
            center = jnp.sum(total, axis=0, keepdims=True)
            both = None
            for part in PARTS:
                dscore = (probs[k, h, part] * (slopes[h, part] - center)).astype(jnp.bfloat16)
                share = jnp.dot(kcs[h, clip, :, part], dscore, preferred_element_type=jnp.float32)
                both = share if both is None else both + share
            both = both * FACTOR
            ul, uh, wl, wh = (both[i * HALF : (i + 1) * HALF] for i in range(4))
            gain = gk[h]
            gl, gh = gain[:HALF], gain[HALF:]
            dl, dh = gl * ul - gh * wh, gl * wl + gh * uh
            hat = qhat[k, h]
            rot = qrot[k, h].astype(jnp.float32)
            ql, qh = rot[:HALF], rot[HALF:]
            acc[2 * h, :HALF] += (dl * cs + dh * sn) * hat[:HALF]
            acc[2 * h, HALF:] += ql * ul + qh * wl
            acc[2 * h + 1, :HALF] += (dh * cs - dl * sn) * hat[HALF:]
            acc[2 * h + 1, HALF:] += qh * uh - ql * wh

    each(1, 8, lambda k: arrival(C, k).wait_recv())
    loop(0, 8, grad_span)

    def far_query(k):
        arrival(Q, k).wait_recv()
        query_span(k)

    loop(8, N_SEQ, far_query)

    def far_grad(k):
        arrival(C, k).wait_recv()
        grad_span(k)

    loop(8, N_SEQ, far_grad)

    for i in range(4):
        sums[i] = jnp.sum(acc[i].T, axis=0, keepdims=True)
    each(0, N_DP - 1, lambda i: send_acc(i).start())
    red[N_DP - 1 : N_DP] = sums[pl.ds(y, 1)]

    def wait_sends(k):
        send_stat(k).wait_send()
        for a in range(4):
            send(a, k).wait_send()

    each(1, N_SEQ, wait_sends)
    each(0, N_DP - 1, lambda i: send_acc(i).wait_send())
    each(0, N_DP - 1, lambda i: arrival_acc(i).wait_recv())
    total = jnp.broadcast_to(jnp.sum(red[...], axis=0), (8, SPAN))
    mine = pltpu.roll(total, (SPAN - 8 * z) % SPAN, 1)
    out[...] = mine[0:1]


def on_device(cos, sin, q_in, k_in, v_in, cotangent, owner, gain_q, gain_k):
    bf16, f32, dma = jnp.bfloat16, jnp.float32, pltpu.SemaphoreType.DMA
    anywhere = pl.BlockSpec(memory_space=pl.ANY)
    in_vmem = pl.BlockSpec(memory_space=pltpu.VMEM)
    span_buf = pltpu.VMEM((N_SEQ, SPAN, WIDTH), bf16)
    out = pl.pallas_call(
        kernel,
        out_shape=jax.ShapeDtypeStruct((1, SPAN), f32),
        in_specs=[anywhere] * 9,
        out_specs=in_vmem,
        scratch_shapes=[
            span_buf, span_buf, span_buf, span_buf,
            pltpu.VMEM((2, SPAN, HD_ALL), bf16),
            pltpu.VMEM((2, SPAN), f32),
            pltpu.VMEM((N_SEQ, 2, SPAN), f32),
            pltpu.VMEM((SPANS_CLIP, HALF, SPAN), f32),
            pltpu.VMEM((SPANS_CLIP, HALF, SPAN), f32),
            pltpu.VMEM((2, LOCAL_HEADS, HEAD_DIM), f32),
            pltpu.VMEM((LOCAL_HEADS, HEAD_DIM, SPAN), f32),
            pltpu.VMEM((LOCAL_HEADS, HEAD_DIM, SPAN), f32),
            pltpu.VMEM((LOCAL_HEADS, 2, CLIP, HEAD_DIM), bf16),
            pltpu.VMEM((LOCAL_HEADS, 2, 2 * HEAD_DIM, CLIP), bf16),
            pltpu.VMEM((LOCAL_HEADS, 2, CLIP, HEAD_DIM), bf16),
            pltpu.VMEM((N_SEQ, LOCAL_HEADS, HEAD_DIM, SPAN), f32),
            pltpu.VMEM((N_SEQ, LOCAL_HEADS, HEAD_DIM, SPAN), bf16),
            pltpu.VMEM((N_SEQ, LOCAL_HEADS, CLIP, SPAN), f32),
            pltpu.VMEM((LOCAL_HEADS, CLIP, SPAN), f32),
            pltpu.VMEM((4, SPAN, SPAN), f32),
            pltpu.VMEM((4, 1, SPAN), f32),
            pltpu.VMEM((N_DP, 1, SPAN), f32),
            pltpu.SMEM((N_SEQ,), jnp.int32),
            pltpu.SMEM((N_SEQ,), jnp.int32),
            pltpu.SMEM((1, N_SEQ), jnp.int32),
            dma((4, N_SEQ)), dma((4, N_SEQ)),
            dma((N_SEQ,)), dma((N_SEQ,)),
            dma((N_DP,)), dma((N_DP,)),
            dma((4,)), dma((7,)),
        ],
        compiler_params=pltpu.CompilerParams(
            collective_id=0, has_side_effects=True, vmem_limit_bytes=56 * 2**20
        ),
    )(
        owner, cos, sin, gain_q.reshape(LOCAL_HEADS, HEAD_DIM), gain_k.reshape(LOCAL_HEADS, HEAD_DIM),
        q_in, k_in, v_in, cotangent,
    )
    return out[0, 0:8], out[0, HALF : HALF + 8]


def solution(mesh):
    cos, sin = rope_constants()
    mapped = jax.shard_map(
        on_device,
        mesh=mesh,
        in_specs=(
            P(), P(),
            P(("dp", "seq"), None),
            P(("dp", "seq"), None),
            P(("dp", "seq"), None),
            P(("dp", "seq"), None),
            P("dp", None),
            P("seq"),
            P("seq"),
        ),
        out_specs=(P(("seq", "dp")), P(("seq", "dp"))),
        check_vma=False,
    )
    return lambda *args: mapped(jnp.asarray(cos), jnp.asarray(sin), *args)
```
